256 devices in a mesh: ctx: 32 (over z, y), head: 8 (over x, core).
Axes of the slice: x: 4, y: 4, z: 8, core: 2. Of those that a mesh axis runs over, the one named last changes fastest.
Arguments:
- queries: bfloat16 [65536, 2048], P('ctx', 'head'), may hold values from -6 to 6
- keys: bfloat16 [65536, 2048], P('ctx', 'head'), may hold values from -6 to 6
- values: bfloat16 [65536, 2048], P('ctx', 'head'), may hold values from -6 to 6
- chosen: int32 [256, 3], P('ctx'), may hold values from 0 to 254, as said below
- w_out: bfloat16 [2048, 4096], P('head'), may hold values from -0.1875 to 0.1875
Outputs:
- mixed: bfloat16 [65536, 4096], P('ctx', 'head')
The draws below stay inside these ranges and needn't reach their ends.
Inputs may be any that keep to these rules, and one draw needn't show every extreme that they name: Every entry of row j is at most j; the three entries of a row differ unless they equal j. For each pair of devices, the query blocks of the later device choose at most one key block of the earlier device, and it is the same block for all of them (the device's own earlier blocks are not so bound); no block of a later device is chosen.
All inputs are finite; a program needn't handle non-finite values.
Results may differ from the reference program's by a relative error of at most 0.023.
Values may be sent and summed in bfloat16 or wider, within the bound.
No kernel may reach another device: no remote copies, remote signals or barrier semaphores. Data moves between devices by JAX's collectives and lax.ppermute only.
A program may use at most 128 MiB of HBM per device.

```python
import jax
import jax.numpy as jnp
from jax import lax

D = 4096
HEADS = 16
HD = 128
BLK = 256
TOK_DEV = 2048
TOKENS = 65536
NBLK = 256
HEAD_DEV = 2


def draw_queries(key, part):
    key = jax.random.fold_in(key, 1)
    baseline_sample = jnp.clip(jax.random.normal(key, (TOKENS, HEADS * HD), jnp.float32), -6.0, 6.0)
    return baseline_sample.astype(jnp.bfloat16)


def draw_keys(key, part):
    key = jax.random.fold_in(key, 2)
    baseline_sample = jnp.clip(jax.random.normal(key, (TOKENS, HEADS * HD), jnp.float32), -6.0, 6.0)
    return baseline_sample.astype(jnp.bfloat16)


def draw_chosen(key, part):
    key = jax.random.fold_in(key, 7)
    first_key, second_key = jax.random.split(key)
    total_block_count = TOKENS // BLK
    per_device = TOK_DEV // BLK
    device_count = TOKENS // TOK_DEV
    designated = jax.random.randint(first_key, (device_count, device_count), 0, per_device)
    query_block = jnp.arange(total_block_count)[:, None]
    current_key_block = jnp.arange(total_block_count)[None, :]
    query_dev = query_block // per_device
    key_dev = current_key_block // per_device
    marked = designated[query_dev, key_dev] == current_key_block % per_device
    distant_allowed = marked & (key_dev < query_dev)
    local_ok = (key_dev == query_dev) & (current_key_block < query_block)
    prior_block = local_ok & (current_key_block == query_block - 1)
    baseline_sample = jax.random.randint(second_key, (total_block_count, total_block_count), 0, 4096)
    extra_score = jnp.where(prior_block, 8192, jnp.where(distant_allowed, 3072, 0))
    logit_scores = (baseline_sample + extra_score) * total_block_count + current_key_block
    logit_scores = jnp.where(distant_allowed | local_ok, logit_scores, -1)
    top_values, top_index = lax.top_k(logit_scores, 3)
    return jnp.where(top_values >= 0, top_index, query_block).astype(jnp.int32)


def raised(values, rng, source, target, blocks, factor):
    def block_of(dim):
        return (jnp.arange(values.shape[dim]) // (values.shape[dim] // blocks)).reshape((-1,) + (1,) * (values.ndim - 1 - dim))

    one_side = jax.random.permutation(rng, blocks)[block_of(target)]
    other_side = (block_of(target) + blocks // 2) % blocks
    return jnp.where((block_of(source) == one_side) | (block_of(source) == other_side), factor * values, values)


def level_of(key, shape, cuts, least, largest):
    gain = 1.0
    for dim, blocks in cuts:
        draws = jax.random.uniform(jax.random.fold_in(jax.random.fold_in(key, 6), dim), (blocks,), jnp.float32, least / len(cuts), largest / len(cuts))
        gain = gain * jnp.repeat(jnp.exp(draws), shape[dim] // blocks).reshape((-1,) + (1,) * (len(shape) - 1 - dim))
    return gain


def noise(stream_key, shape, spread, most, cuts=(), kind=jnp.bfloat16):
    values = spread * jax.random.normal(stream_key, shape, jnp.float32)
    if cuts:
        values = values * level_of(stream_key, shape, cuts, -0.22, 0.18)
    return jnp.clip(values, -most, most).astype(kind)


def bell_draw_with(own_key, shape, deviation, most, cuts, heavy, dtype=jnp.bfloat16):
    array = deviation * jax.random.normal(own_key, shape, jnp.float32)
    if cuts:
        array = array * level_of(own_key, shape, cuts, -0.22, 0.18)
    return jnp.clip(raised(array, jax.random.fold_in(own_key, 3), *heavy), -most, most).astype(dtype)


def setup_inputs(seed: int = 0) -> dict:
    streams_of = jax.random.split(jax.random.key(seed), 6)
    return {
        "queries": draw_queries(jax.random.fold_in(streams_of[5], 71), 0),
        "keys": draw_keys(jax.random.fold_in(streams_of[5], 71), 0),
        "values": noise(streams_of[2], (TOKENS, HEADS * HD), 1.0, 6.0, ((0, 32), (1, 8))),
        "chosen": draw_chosen(jax.random.fold_in(streams_of[5], 71), 0),
        "w_out": bell_draw_with(streams_of[4], (HEADS * HD, D), (HEADS * HD) ** -0.5, 0.1875, ((0, 8),), (0, 1, 8, 2.0)),
    }


def reference(queries, keys, values, chosen, w_out):
    query_blocks = queries.reshape(NBLK, BLK, HEADS, HD)
    key_blocks = keys.reshape(NBLK, BLK, HEADS, HD)
    value_blocks = values.reshape(NBLK, BLK, HEADS, HD)
    positions = jnp.arange(BLK)
    causal = positions[None, :] <= positions[:, None]
    group_width = HEAD_DEV * HD
    groups = HEADS // HEAD_DEV
    out_groups = w_out.reshape(groups, group_width, D)

    def attend_block(block_index):
        picks = chosen[block_index]
        key_set = jnp.concatenate([key_blocks[block_index], key_blocks[picks[0]], key_blocks[picks[1]], key_blocks[picks[2]]], 0).astype(jnp.float32)
        value_set = jnp.concatenate([value_blocks[block_index], value_blocks[picks[0]], value_blocks[picks[1]], value_blocks[picks[2]]], 0).astype(jnp.float32)
        logit_scores = jnp.einsum("qhd,khd->hqk", query_blocks[block_index].astype(jnp.float32), key_set) * (HD ** -0.5)
        live_parts = [jnp.broadcast_to(picks[slot] != block_index, (BLK, BLK)) for slot in range(3)]
        mask = jnp.concatenate([causal] + live_parts, 1)
        logit_scores = jnp.where(mask[None], logit_scores, -jnp.inf)
        row_max = jnp.max(logit_scores, axis=-1, keepdims=True)
        exp_scores = jnp.exp(logit_scores - row_max)
        row_total = jnp.sum(exp_scores, axis=-1, keepdims=True)
        weights = (exp_scores / row_total).astype(jnp.bfloat16)
        attended = jnp.einsum("hqk,khd->qhd", weights.astype(jnp.float32), value_set).astype(jnp.bfloat16)
        attended = attended.reshape(BLK, groups, group_width)
        running = jnp.zeros((BLK, D), jnp.float32)
        for group_index in range(groups):
            group_part = jnp.dot(attended[:, group_index], out_groups[group_index], preferred_element_type=jnp.float32).astype(jnp.bfloat16)
            running = running + lax.optimization_barrier(group_part).astype(jnp.float32)
        return running.astype(jnp.bfloat16)

    mixed = lax.map(attend_block, jnp.arange(NBLK))
    return mixed.reshape(TOKENS, D)
```

```python
import functools

import jax
import jax.numpy as jnp
from jax import lax
from jax.experimental import pallas as pl
from jax.experimental.pallas import tpu as pltpu
from jax.sharding import PartitionSpec as P

HD = 128
BLK = 256
SCALE = HD ** (-0.5) * 1.4426950408889634


def attend_kernel(head, blocks_here, slot_ref, live_ref, q_ref, k_hbm, v_hbm, in_hbm, o_ref, kpool, vpool, sems):
    j = pl.program_id(0)
    peers = in_hbm.shape[0]
    cols = pl.ds(head * HD, HD)
    copies = [
        pltpu.make_async_copy(k_hbm.at[:, :, cols], kpool.at[pl.ds(0, blocks_here)], sems.at[0]),
        pltpu.make_async_copy(in_hbm.at[:, 0], kpool.at[pl.ds(blocks_here, peers)], sems.at[1]),
        pltpu.make_async_copy(v_hbm.at[:, :, cols], vpool.at[pl.ds(0, blocks_here), :, pl.ds(0, HD)], sems.at[2]),
        pltpu.make_async_copy(in_hbm.at[:, 1], vpool.at[pl.ds(blocks_here, peers), :, pl.ds(0, HD)], sems.at[3]),
    ]

    @pl.when(j == 0)
    def _():
        for copy in copies:
            copy.start()

        def fill(i, carry):
            vpool[i, :, pl.ds(HD, HD)] = jnp.ones((BLK, HD), jnp.bfloat16)
            return carry

        lax.fori_loop(0, blocks_here + peers, fill, 0)
        for copy in copies:
            copy.wait()

    q = q_ref[...]
    nt = (((1,), (1,)), ((), ()))
    slots = [j] + [slot_ref[j, p] for p in range(3)]
    scores = [lax.dot_general(q, kpool[s], nt, preferred_element_type=jnp.float32) for s in slots]
    rows = lax.broadcasted_iota(jnp.int32, (BLK, BLK), 0)
    keys = lax.broadcasted_iota(jnp.int32, (BLK, BLK), 1)
    scores[0] = jnp.where(keys <= rows, scores[0], -jnp.inf)
    for p in range(3):
        scores[p + 1] = scores[p + 1] + jnp.where(live_ref[j, p] != 0, 0.0, -jnp.inf)
    top = jnp.maximum(jnp.maximum(scores[0], scores[1]), jnp.maximum(scores[2], scores[3]))
    top = jnp.max(top, axis=1, keepdims=True) * SCALE
    total = None
    for s, sc in zip(slots, scores):
        w = jnp.exp2(sc * SCALE - top).astype(jnp.bfloat16)
        term = jnp.dot(w, vpool[s], preferred_element_type=jnp.float32)
        total = term if total is None else total + term
    o_ref[...] = (total[:, :HD] / total[:, HD:]).astype(jnp.bfloat16)


def attend(head, slots, live, queries, kb, vb, incoming):
    rows = queries.shape[0]
    blocks_here = rows // BLK
    pool = blocks_here + incoming.shape[0]
    return pl.pallas_call(
        functools.partial(attend_kernel, head, blocks_here),
        out_shape=jax.ShapeDtypeStruct((rows, HD), jnp.bfloat16),
        grid_spec=pltpu.PrefetchScalarGridSpec(
            num_scalar_prefetch=2,
            grid=(blocks_here,),
            in_specs=[
                pl.BlockSpec((BLK, HD), lambda j, *_: (j, head)),
                pl.BlockSpec(memory_space=pl.ANY),
                pl.BlockSpec(memory_space=pl.ANY),
                pl.BlockSpec(memory_space=pl.ANY),
            ],
            out_specs=pl.BlockSpec((BLK, HD), lambda j, *_: (j, 0)),
            scratch_shapes=[
                pltpu.VMEM((pool, BLK, HD), jnp.bfloat16),
                pltpu.VMEM((pool, BLK, 2 * HD), jnp.bfloat16),
                pltpu.SemaphoreType.DMA((4,)),
            ],
        ),
        compiler_params=pltpu.CompilerParams(vmem_limit_bytes=40 * 1024 * 1024),
        cost_estimate=pl.CostEstimate(
            flops=4 * rows * 4 * BLK * HD, bytes_accessed=pool * BLK * HD * 4, transcendentals=rows * 4 * BLK
        ),
    )(slots, live, queries, kb, vb, incoming)


def on_device(queries, keys, values, chosen, w_out):
    row_count, feature_width = queries.shape
    blocks_here = row_count // BLK
    heads_here = feature_width // HD
    device_count = lax.axis_size("ctx")
    my_index = lax.axis_index("ctx")

    table = lax.all_gather(chosen, "ctx", axis=0, tiled=True).reshape(device_count, -1)
    asked = jnp.max(jnp.where(table // blocks_here == my_index, table % blocks_here, 0), axis=1)

    owner_dev = chosen // blocks_here
    own_block = my_index * blocks_here + jnp.arange(blocks_here, dtype=jnp.int32)[:, None]
    live = (chosen != own_block).astype(jnp.int32)
    slots = jnp.where(owner_dev == my_index, chosen % blocks_here, blocks_here + owner_dev)

    kb = keys.reshape(blocks_here, BLK, feature_width)
    vb = values.reshape(blocks_here, BLK, feature_width)
    incoming = []
    for head in range(heads_here):
        cols = slice(head * HD, (head + 1) * HD)
        pair = jnp.stack([kb[:, :, cols], vb[:, :, cols]], axis=1)
        incoming.append(lax.all_to_all(pair[asked], "ctx", split_axis=0, concat_axis=0, tiled=True))

    w_cols = lax.all_to_all(w_out, "head", split_axis=1, concat_axis=0, tiled=True)
    groups = lax.axis_size("head")
    w_cols = w_cols.reshape(groups, heads_here, HD, -1)
    total = None
    for head in range(heads_here):
        attended = attend(head, slots, live, queries, kb, vb, incoming[head])
        gathered = lax.all_gather(attended, "head", axis=1, tiled=True)
        term = jnp.dot(gathered, w_cols[:, head].reshape(groups * HD, -1), preferred_element_type=jnp.float32)
        total = term if total is None else total + term
    return total.astype(jnp.bfloat16)


def solution(mesh):
    in_specs = (
        P("ctx", "head"),
        P("ctx", "head"),
        P("ctx", "head"),
        P("ctx", None),
        P("head", None),
    )
    out_specs = P("ctx", "head")
    return jax.shard_map(
        on_device, mesh=mesh, in_specs=in_specs, out_specs=out_specs, check_vma=False
    )
```

```python
import functools

import jax
import jax.numpy as jnp
from jax import lax
from jax.experimental import pallas as pl
from jax.experimental.pallas import tpu as pltpu
from jax.sharding import PartitionSpec as P

HD = 128
NZ, NY = 8, 4
BLK = 256
SCALE = HD ** (-0.5) * 1.4426950408889634


def attend_kernel(head, blocks_here, layout, slot_ref, live_ref, *refs):
    q_ref, k_hbm, v_hbm = refs[:3]
    n = len(layout)
    parts = refs[3 : 3 + n]
    o_ref, kpool, vpool, sems = refs[3 + n :]
    j = pl.program_id(0)
    cols = pl.ds(head * HD, HD)
    mine = slot_ref[blocks_here, 0]
    copies = [
        pltpu.make_async_copy(k_hbm.at[:, :, cols], kpool.at[pl.ds(0, blocks_here)], sems.at[0]),
        pltpu.make_async_copy(v_hbm.at[:, :, cols], vpool.at[pl.ds(0, blocks_here), :, pl.ds(0, HD)], sems.at[1]),
    ]
    for i, (part, (slot, own)) in enumerate(zip(parts, layout)):
        at = pl.ds(blocks_here + slot, 1)
        block = pl.ds(mine if own else 0, 1)
        copies.append(pltpu.make_async_copy(part.at[block, 0], kpool.at[at], sems.at[2 + 2 * i]))
        copies.append(
            pltpu.make_async_copy(part.at[block, 1], vpool.at[at, :, pl.ds(0, HD)], sems.at[3 + 2 * i])
        )

    @pl.when(j == 0)
    def _():
        for copy in copies:
            copy.start()

        def fill(i, carry):
            vpool[i, :, pl.ds(HD, HD)] = jnp.ones((BLK, HD), jnp.bfloat16)
            return carry

        lax.fori_loop(0, vpool.shape[0], fill, 0)
        for copy in copies:
            copy.wait()

    q = q_ref[...]
    nt = (((1,), (1,)), ((), ()))
    slots = [j] + [slot_ref[j, p] for p in range(3)]
    scores = [lax.dot_general(q, kpool[s], nt, preferred_element_type=jnp.float32) for s in slots]
    rows = lax.broadcasted_iota(jnp.int32, (BLK, BLK), 0)
    keys = lax.broadcasted_iota(jnp.int32, (BLK, BLK), 1)
    scores[0] = jnp.where(keys <= rows, scores[0], -jnp.inf)
    for p in range(3):
        scores[p + 1] = scores[p + 1] + jnp.where(live_ref[j, p] != 0, 0.0, -jnp.inf)
    top = jnp.maximum(jnp.maximum(scores[0], scores[1]), jnp.maximum(scores[2], scores[3]))
    top = jnp.max(top, axis=1, keepdims=True) * SCALE
    total = None
    for s, sc in zip(slots, scores):
        w = jnp.exp2(sc * SCALE - top).astype(jnp.bfloat16)
        term = jnp.dot(w, vpool[s], preferred_element_type=jnp.float32)
        total = term if total is None else total + term
    o_ref[...] = (total[:, :HD] / total[:, HD:]).astype(jnp.bfloat16)


def attend(head, slots, live, queries, kb, vb, parts):
    rows = queries.shape[0]
    blocks_here = rows // BLK
    layout = [(slot, own) for slot, own, _ in parts]
    arrays = [array for _, _, array in parts]
    pool = blocks_here + NZ * NY
    return pl.pallas_call(
        functools.partial(attend_kernel, head, blocks_here, layout),
        out_shape=jax.ShapeDtypeStruct((rows, HD), jnp.bfloat16),
        grid_spec=pltpu.PrefetchScalarGridSpec(
            num_scalar_prefetch=2,
            grid=(blocks_here,),
            in_specs=[pl.BlockSpec((BLK, HD), lambda j, *_: (j, head))]
            + [pl.BlockSpec(memory_space=pl.ANY)] * (2 + len(arrays)),
            out_specs=pl.BlockSpec((BLK, HD), lambda j, *_: (j, 0)),
            scratch_shapes=[
                pltpu.VMEM((pool, BLK, HD), jnp.bfloat16),
                pltpu.VMEM((pool, BLK, 2 * HD), jnp.bfloat16),
                pltpu.SemaphoreType.DMA((2 + 2 * len(arrays),)),
            ],
        ),
        compiler_params=pltpu.CompilerParams(vmem_limit_bytes=40 * 1024 * 1024),
        cost_estimate=pl.CostEstimate(
            flops=4 * rows * 4 * BLK * HD, bytes_accessed=pool * BLK * HD * 4, transcendentals=rows * 4 * BLK
        ),
    )(slots, live, queries, kb, vb, *arrays)


def along_z(x, step, senders):
    pairs = [
        (z * NY + y, (z + step) % NZ * NY + y) for z in senders for y in range(NY)
    ]
    return lax.ppermute(x, "ctx", pairs)


def along_y(x, shift, wrap, zs):
    pairs = [
        (z * NY + y, z * NY + (y + shift) % NY)
        for z in zs
        for y in range(NY)
        if wrap or y + shift < NY
    ]
    return lax.ppermute(x, "ctx", pairs)


def exchange(own, need, z, y):
    def wanted(dest, src):
        rows = lax.dynamic_index_in_dim(need, dest % NZ, 0, False)
        rows = lax.dynamic_index_in_dim(rows, src % NZ, 1, False)
        return lax.dynamic_index_in_dim(rows, y, 1, False)

    f1 = along_z(own, 1, range(7))
    b1 = along_z(own, -1, (0, 1, 2))
    f2 = along_z(f1, 1, range(1, 7))
    b2 = along_z(b1, -1, (7, 0, 1))
    f3 = along_z(f2, 1, (2, 3, 5))
    f3s = along_z(f2[wanted(z + 1, z - 2)], 1, (4, 6))
    b3 = along_z(b2, -1, (6, 0))
    b3s = along_z(b2[wanted(z - 1, z + 2)], -1, (7,))
    f4s = along_z(f3[wanted(z + 1, z - 3)], 1, (4, 6))
    b4s = along_z(b3[wanted(z - 1, z + 3)], -1, (5, 7))

    got = {
        0: own[wanted(z, z)],
        1: f1[wanted(z, z - 1)],
        2: f2[wanted(z, z - 2)],
        3: jnp.where((z == 5) | (z == 7), f3s, f3[wanted(z, z - 3)]),
        4: jnp.where((z == 5) | (z == 7), f4s, b4s),
        5: jnp.where(z == 6, b3s, b3[wanted(z, z - 5)]),
        6: b2[wanted(z, z - 6)],
        7: b1[wanted(z, z - 7)],
    }
    parts = []
    for k in (0, 1, 2, 7, 6, 3, 5, 4):
        if k:
            parts.append((k * NY, True, got[k]))
        for shift in range(1, NY):
            item = lax.dynamic_index_in_dim(got[k], (y + shift) % NY, 0, True)
            parts.append((k * NY + shift, False, along_y(item, shift, k > 0, range(k, NZ))))
    return parts


def on_device(queries, keys, values, chosen, w_out):
    row_count, feature_width = queries.shape
    blocks_here = row_count // BLK
    heads_here = feature_width // HD
    device_count = lax.axis_size("ctx")
    my_index = lax.axis_index("ctx")
    z, y = my_index // NY, my_index % NY

    spread = jnp.broadcast_to(chosen.reshape(1, -1), (device_count, chosen.size))
    table = lax.all_to_all(spread, "ctx", split_axis=0, concat_axis=0, tiled=True)
    devices = jnp.arange(device_count, dtype=jnp.int32)
    hit = table[:, :, None] // blocks_here == devices
    need = jnp.max(jnp.where(hit, table[:, :, None] % blocks_here, 0), axis=1)
    need = need.reshape(NZ, NY, NZ, NY)

    owner_dev = chosen // blocks_here
    own_block = my_index * blocks_here + jnp.arange(blocks_here, dtype=jnp.int32)[:, None]
    live = (chosen != own_block).astype(jnp.int32)
    far = blocks_here + (z - owner_dev // NY) * NY + (y - owner_dev) % NY
    slots = jnp.where(owner_dev == my_index, chosen % blocks_here, far)
    slots = jnp.concatenate([slots, jnp.broadcast_to(y, (1, 3))], axis=0)

    kb = keys.reshape(blocks_here, BLK, feature_width)
    vb = values.reshape(blocks_here, BLK, feature_width)
    w_cols = lax.all_to_all(w_out, "head", split_axis=1, concat_axis=0, tiled=True)
    groups = lax.axis_size("head")
    total = None
    for head in range(heads_here):
        cols = slice(head * HD, (head + 1) * HD)
        pair = jnp.stack([kb[:, :, cols], vb[:, :, cols]], axis=1)
        parts = exchange(pair, need, z, y)
        if head == 0:
            live, w_cols = lax.optimization_barrier((live, w_cols))
            w_cols = w_cols.reshape(groups, heads_here, HD, -1)
        attended = attend(head, slots, live, queries, kb, vb, parts)
        gathered = lax.all_gather(attended, "head", axis=1, tiled=True)
        term = jnp.dot(gathered, w_cols[:, head].reshape(groups * HD, -1), preferred_element_type=jnp.float32)
        total = term if total is None else total + term
    return total.astype(jnp.bfloat16)


def solution(mesh):
    in_specs = (
        P("ctx", "head"),
        P("ctx", "head"),
        P("ctx", "head"),
        P("ctx", None),
        P("head", None),
    )
    out_specs = P("ctx", "head")
    return jax.shard_map(
        on_device, mesh=mesh, in_specs=in_specs, out_specs=out_specs, check_vma=False
    )
```

```python
import functools

import jax
import jax.numpy as jnp
from jax import lax
from jax.experimental import pallas as pl
from jax.experimental.pallas import tpu as pltpu
from jax.sharding import PartitionSpec as P

HD = 128
BLK = 256
UNROLL = 2
SCALE = HD ** (-0.5) * 1.4426950408889634


def attend_kernel(head, blocks_here, slot_ref, live_ref, q_ref, k_hbm, v_hbm, in_hbm, o_ref, kpool, vpool, sems):
    j = pl.program_id(0)
    peers = in_hbm.shape[0]
    cols = pl.ds(head * HD, HD)
    copies = [
        pltpu.make_async_copy(k_hbm.at[:, :, cols], kpool.at[pl.ds(0, blocks_here)], sems.at[0]),
        pltpu.make_async_copy(in_hbm.at[:, 0], kpool.at[pl.ds(blocks_here, peers)], sems.at[1]),
        pltpu.make_async_copy(v_hbm.at[:, :, cols], vpool.at[pl.ds(0, blocks_here), :, pl.ds(0, HD)], sems.at[2]),
        pltpu.make_async_copy(in_hbm.at[:, 1], vpool.at[pl.ds(blocks_here, peers), :, pl.ds(0, HD)], sems.at[3]),
    ]

    @pl.when(j == 0)
    def _():
        for copy in copies:
            copy.start()

        def fill(i, carry):
            vpool[i, :, pl.ds(HD, HD)] = jnp.ones((BLK, HD), jnp.bfloat16)
            return carry

        lax.fori_loop(0, blocks_here + peers, fill, 0)
        for copy in copies:
            copy.wait()

    nt = (((1,), (1,)), ((), ()))
    rows = lax.broadcasted_iota(jnp.int32, (BLK, BLK), 0)
    keys = lax.broadcasted_iota(jnp.int32, (BLK, BLK), 1)
    for u in range(UNROLL):
        block = j * UNROLL + u
        at = pl.ds(u * BLK, BLK)
        q = q_ref[at, :]
        slots = [block] + [slot_ref[block, p] for p in range(3)]
        scores = [lax.dot_general(q, kpool[s], nt, preferred_element_type=jnp.float32) for s in slots]
        scores[0] = jnp.where(keys <= rows, scores[0], -jnp.inf)
        for p in range(3):
            scores[p + 1] = scores[p + 1] + jnp.where(live_ref[block, p] != 0, 0.0, -jnp.inf)
        top = jnp.maximum(jnp.maximum(scores[0], scores[1]), jnp.maximum(scores[2], scores[3]))
        top = jnp.max(top, axis=1, keepdims=True) * SCALE
        total = None
        for s, sc in zip(slots, scores):
            w = jnp.exp2(sc * SCALE - top).astype(jnp.bfloat16)
            term = jnp.dot(w, vpool[s], preferred_element_type=jnp.float32)
            total = term if total is None else total + term
        o_ref[at, :] = (total[:, :HD] / total[:, HD:]).astype(jnp.bfloat16)


def attend(head, slots, live, queries, kb, vb, incoming):
    rows = queries.shape[0]
    blocks_here = rows // BLK
    pool = blocks_here + incoming.shape[0]
    return pl.pallas_call(
        functools.partial(attend_kernel, head, blocks_here),
        out_shape=jax.ShapeDtypeStruct((rows, HD), jnp.bfloat16),
        grid_spec=pltpu.PrefetchScalarGridSpec(
            num_scalar_prefetch=2,
            grid=(blocks_here // UNROLL,),
            in_specs=[
                pl.BlockSpec((UNROLL * BLK, HD), lambda j, *_: (j, head)),
                pl.BlockSpec(memory_space=pl.ANY),
                pl.BlockSpec(memory_space=pl.ANY),
                pl.BlockSpec(memory_space=pl.ANY),
            ],
            out_specs=pl.BlockSpec((UNROLL * BLK, HD), lambda j, *_: (j, 0)),
            scratch_shapes=[
                pltpu.VMEM((pool, BLK, HD), jnp.bfloat16),
                pltpu.VMEM((pool, BLK, 2 * HD), jnp.bfloat16),
                pltpu.SemaphoreType.DMA((4,)),
            ],
        ),
        compiler_params=pltpu.CompilerParams(vmem_limit_bytes=40 * 1024 * 1024),
        cost_estimate=pl.CostEstimate(
            flops=4 * rows * 4 * BLK * HD, bytes_accessed=pool * BLK * HD * 4, transcendentals=rows * 4 * BLK
        ),
    )(slots, live, queries, kb, vb, incoming)


def shifted(x, shift):
    n = lax.axis_size("head")
    return lax.ppermute(x, "head", [(i, (i + shift) % n) for i in range(n)])


def swapped(x):
    return lax.ppermute(x, "head", [(i, i ^ 1) for i in range(lax.axis_size("head"))])


def project_kernel(half, place_ref, a0, a1, a2, top, bottom, b0, b1, b2, btop, bbottom, w_ref, part_ref, o_ref):
    first = pl.program_id(0) < half
    far = jnp.where(first, top[...], bottom[...])
    bfar = jnp.where(first, btop[...], bbottom[...])
    pieces = [a0[...], a1[...], a2[...], far, b0[...], b1[...], b2[...], bfar]
    rows = [w_ref[place_ref[i]] for i in range(8)]
    x = jnp.concatenate(pieces, axis=1)
    w = jnp.concatenate(rows, axis=0)
    o_ref[...] = (part_ref[...] + jnp.dot(x, w, preferred_element_type=jnp.float32)).astype(jnp.bfloat16)


def project(place, pieces, w, part):
    rows, width = part.shape
    tile = 256
    steps = rows // tile
    half = steps // 2
    full = pl.BlockSpec((tile, HD), lambda i, *_: (i, 0))
    low = pl.BlockSpec((tile, HD), lambda i, *_: (jnp.minimum(i, half - 1), 0))
    high = pl.BlockSpec((tile, HD), lambda i, *_: (jnp.maximum(i - half, 0), 0))
    return pl.pallas_call(
        functools.partial(project_kernel, half),
        out_shape=jax.ShapeDtypeStruct((rows, width), jnp.bfloat16),
        grid_spec=pltpu.PrefetchScalarGridSpec(
            num_scalar_prefetch=1,
            grid=(steps,),
            in_specs=[full, full, full, low, high] * 2
            + [
                pl.BlockSpec(w.shape, lambda i, *_: (0, 0, 0)),
                pl.BlockSpec((tile, width), lambda i, *_: (i, 0)),
            ],
            out_specs=pl.BlockSpec((tile, width), lambda i, *_: (i, 0)),
        ),
        compiler_params=pltpu.CompilerParams(vmem_limit_bytes=32 * 1024 * 1024),
        cost_estimate=pl.CostEstimate(
            flops=2 * rows * 8 * HD * width, bytes_accessed=rows * (8 * HD * 2 + 6 * width), transcendentals=0
        ),
    )(place, *pieces, w, part)


def on_device(queries, keys, values, chosen, w_out):
    row_count, feature_width = queries.shape
    blocks_here = row_count // BLK
    heads_here = feature_width // HD
    device_count = lax.axis_size("ctx")
    my_index = lax.axis_index("ctx")
    groups = lax.axis_size("head")
    group = lax.axis_index("head")

    spread = jnp.broadcast_to(chosen.reshape(1, -1), (device_count, chosen.size))
    table = lax.all_to_all(spread, "ctx", split_axis=0, concat_axis=0, tiled=True)
    asked = jnp.max(jnp.where(table // blocks_here == my_index, table % blocks_here, 0), axis=1)

    owner_dev = chosen // blocks_here
    own_block = my_index * blocks_here + jnp.arange(blocks_here, dtype=jnp.int32)[:, None]
    live = (chosen != own_block).astype(jnp.int32)
    slots = jnp.where(owner_dev == my_index, chosen % blocks_here, blocks_here + owner_dev)

    kb = keys.reshape(blocks_here, BLK, feature_width)
    vb = values.reshape(blocks_here, BLK, feature_width)
    incoming = []
    for head in range(heads_here):
        cols = slice(head * HD, (head + 1) * HD)
        pair = jnp.stack([kb[:, :, cols], vb[:, :, cols]], axis=1)
        incoming.append(lax.all_to_all(pair[asked], "ctx", split_axis=0, concat_axis=0, tiled=True))

    width = w_out.shape[1] // groups
    w_rel = []
    for shift in range(groups):
        part = lax.dynamic_slice_in_dim(w_out, (group + shift) % groups * width, width, 1)
        w_rel.append(shifted(part, shift) if shift else part)
    w_cols = jnp.stack(w_rel)[(group - jnp.arange(groups)) % groups].reshape(groups, heads_here, HD, width)

    first = attend(0, slots, live, queries, kb, vb, incoming[0])
    gathered = lax.all_gather(first, "head", axis=1, tiled=True)
    part = jnp.dot(gathered, w_cols[:, 0].reshape(groups * HD, width), preferred_element_type=jnp.float32)

    live, part, w1 = lax.optimization_barrier((live, part, w_cols[:, 1]))
    a0 = attend(1, slots, live, queries, kb, vb, incoming[1])
    half = row_count // 2
    a1, a2 = shifted(a0, 2), shifted(a0, -2)
    b0 = swapped(a0)
    top, bottom = shifted(a1[:half], 2), shifted(a2[half:], -2)
    b1, b2 = swapped(a1), swapped(a2)
    btop, bbottom = swapped(top), swapped(bottom)
    mine = [group, group - 2, group + 2, group + 4]
    place = jnp.stack([g % groups for g in mine + [(g % groups) ^ 1 for g in mine]]).astype(jnp.int32)
    return project(place, [a0, a1, a2, top, bottom, b0, b1, b2, btop, bbottom], w1, part)


def solution(mesh):
    in_specs = (
        P("ctx", "head"),
        P("ctx", "head"),
        P("ctx", "head"),
        P("ctx", None),
        P("head", None),
    )
    out_specs = P("ctx", "head")
    return jax.shard_map(
        on_device, mesh=mesh, in_specs=in_specs, out_specs=out_specs, check_vma=False
    )
```

```python
import functools

import jax
import jax.numpy as jnp
from jax import lax
from jax.experimental import pallas as pl
from jax.experimental.pallas import tpu as pltpu
from jax.sharding import PartitionSpec as P

HD = 128
BLK = 256
UNROLL = 2
VMEM = 20 * 1024 * 1024
SCALE = HD ** (-0.5) * 1.4426950408889634


def attend_kernel(head, blocks_here, slot_ref, live_ref, q_ref, k_hbm, v_hbm, in_hbm, o_ref, kpool, vpool, sems):
    j = pl.program_id(0)
    peers = in_hbm.shape[0]
    cols = pl.ds(head * HD, HD)
    copies = [
        pltpu.make_async_copy(k_hbm.at[:, :, cols], kpool.at[pl.ds(0, blocks_here)], sems.at[0]),
        pltpu.make_async_copy(in_hbm.at[:, 0], kpool.at[pl.ds(blocks_here, peers)], sems.at[1]),
        pltpu.make_async_copy(v_hbm.at[:, :, cols], vpool.at[pl.ds(0, blocks_here), :, pl.ds(0, HD)], sems.at[2]),
        pltpu.make_async_copy(in_hbm.at[:, 1], vpool.at[pl.ds(blocks_here, peers), :, pl.ds(0, HD)], sems.at[3]),
    ]

    @pl.when(j == 0)
    def _():
        for copy in copies:
            copy.start()

        def fill(i, carry):
            vpool[i, :, pl.ds(HD, HD)] = jnp.ones((BLK, HD), jnp.bfloat16)
            return carry

        lax.fori_loop(0, blocks_here + peers, fill, 0)
        for copy in copies:
            copy.wait()

    nt = (((1,), (1,)), ((), ()))
    rows = lax.broadcasted_iota(jnp.int32, (BLK, BLK), 0)
    keys = lax.broadcasted_iota(jnp.int32, (BLK, BLK), 1)
    for u in range(UNROLL):
        block = j * UNROLL + u
        at = pl.ds(u * BLK, BLK)
        q = q_ref[at, :]
        slots = [block] + [slot_ref[block, p] for p in range(3)]
        scores = [lax.dot_general(q, kpool[s], nt, preferred_element_type=jnp.float32) for s in slots]
        scores[0] = jnp.where(keys <= rows, scores[0], -jnp.inf)
        for p in range(3):
            scores[p + 1] = scores[p + 1] + jnp.where(live_ref[block, p] != 0, 0.0, -jnp.inf)
        top = jnp.maximum(jnp.maximum(scores[0], scores[1]), jnp.maximum(scores[2], scores[3]))
        top = jnp.max(top, axis=1, keepdims=True) * SCALE
        total = None
        for s, sc in zip(slots, scores):
            w = jnp.exp2(sc * SCALE - top).astype(jnp.bfloat16)
            term = jnp.dot(w, vpool[s], preferred_element_type=jnp.float32)
            total = term if total is None else total + term
        o_ref[at, :] = (total[:, :HD] / total[:, HD:]).astype(jnp.bfloat16)


def attend(head, slots, live, queries, kb, vb, incoming):
    rows = queries.shape[0]
    blocks_here = rows // BLK
    pool = blocks_here + incoming.shape[0]
    return pl.pallas_call(
        functools.partial(attend_kernel, head, blocks_here),
        out_shape=jax.ShapeDtypeStruct((rows, HD), jnp.bfloat16),
        grid_spec=pltpu.PrefetchScalarGridSpec(
            num_scalar_prefetch=2,
            grid=(blocks_here // UNROLL,),
            in_specs=[
                pl.BlockSpec((UNROLL * BLK, HD), lambda j, *_: (j, head)),
                pl.BlockSpec(memory_space=pl.ANY),
                pl.BlockSpec(memory_space=pl.ANY),
                pl.BlockSpec(memory_space=pl.ANY),
            ],
            out_specs=pl.BlockSpec((UNROLL * BLK, HD), lambda j, *_: (j, 0)),
            scratch_shapes=[
                pltpu.VMEM((pool, BLK, HD), jnp.bfloat16),
                pltpu.VMEM((pool, BLK, 2 * HD), jnp.bfloat16),
                pltpu.SemaphoreType.DMA((4,)),
            ],
        ),
        compiler_params=pltpu.CompilerParams(vmem_limit_bytes=VMEM),
        cost_estimate=pl.CostEstimate(
            flops=4 * rows * 4 * BLK * HD, bytes_accessed=pool * BLK * HD * 4, transcendentals=rows * 4 * BLK
        ),
    )(slots, live, queries, kb, vb, incoming)


def shifted(x, shift):
    n = lax.axis_size("head")
    return lax.ppermute(x, "head", [(i, (i + shift) % n) for i in range(n)])


def swapped(x):
    return lax.ppermute(x, "head", [(i, i ^ 1) for i in range(lax.axis_size("head"))])


def gathered_pieces(own):
    half = own.shape[0] // 2
    before, behind = shifted(own, 2), shifted(own, -2)
    own_s = swapped(own)
    top, bottom = shifted(before[:half], 2), shifted(behind[half:], -2)
    before_s, behind_s = swapped(before), swapped(behind)
    top_s, bottom_s = swapped(top), swapped(bottom)
    return [own, before, behind, top, bottom, own_s, before_s, behind_s, top_s, bottom_s]


def project_kernel(tile, *refs):
    pieces, w_ref, rest = refs[:10], refs[10], refs[11:]
    step, steps = pl.program_id(0), pl.num_programs(0)
    first = step < steps // 2
    at = pl.ds(pl.multiple_of(step * tile, tile), tile)
    at_half = pl.ds(pl.multiple_of(step % (steps // 2) * tile, tile), tile)
    ordered = []
    for i in (0, 5):
        a0, a1, a2, top, bottom = pieces[i : i + 5]
        far = jnp.where(first, top[at_half, :], bottom[at_half, :])
        ordered += [a0[at, :], a1[at, :], a2[at, :], far]
    out = jnp.dot(jnp.concatenate(ordered, axis=1), w_ref[...], preferred_element_type=jnp.float32)
    if len(rest) == 2:
        out = out + rest[0][...]
    rest[-1][...] = out.astype(rest[-1].dtype)


def project(pieces, w, part=None):
    rows, width = pieces[0].shape[0], w.shape[1]
    tile = rows // 4
    steps = rows // tile
    wide = pl.BlockSpec((tile, width), lambda i: (i, 0))
    more = [] if part is None else [part]
    return pl.pallas_call(
        functools.partial(project_kernel, tile),
        out_shape=jax.ShapeDtypeStruct((rows, width), jnp.float32 if part is None else jnp.bfloat16),
        grid=(steps,),
        in_specs=[pl.BlockSpec(memory_space=pltpu.VMEM)] * 11 + [wide] * len(more),
        out_specs=wide,
        compiler_params=pltpu.CompilerParams(vmem_limit_bytes=VMEM),
        cost_estimate=pl.CostEstimate(
            flops=2 * rows * w.shape[0] * width, bytes_accessed=rows * (w.shape[0] * 2 + 6 * width), transcendentals=0
        ),
    )(*pieces, w, *more)


def on_device(queries, keys, values, chosen, w_out):
    row_count, feature_width = queries.shape
    blocks_here = row_count // BLK
    heads_here = feature_width // HD
    device_count = lax.axis_size("ctx")
    my_index = lax.axis_index("ctx")
    groups = lax.axis_size("head")
    group = lax.axis_index("head")

    spread = jnp.broadcast_to(chosen[None], (device_count,) + chosen.shape)
    table = lax.all_to_all(spread, "ctx", split_axis=0, concat_axis=0, tiled=True)
    asked = jnp.max(jnp.where(table // blocks_here == my_index, table % blocks_here, 0), axis=(1, 2))

    owner_dev = chosen // blocks_here
    own_block = my_index * blocks_here + jnp.arange(blocks_here, dtype=jnp.int32)[:, None]
    live = (chosen != own_block).astype(jnp.int32)
    slots = jnp.where(owner_dev == my_index, chosen % blocks_here, blocks_here + owner_dev)

    kb = keys.reshape(blocks_here, BLK, feature_width)
    vb = values.reshape(blocks_here, BLK, feature_width)
    incoming = []
    for head in range(heads_here):
        cols = slice(head * HD, (head + 1) * HD)
        pair = jnp.stack([kb[:, :, cols], vb[:, :, cols]], axis=1)
        incoming.append(lax.all_to_all(pair[asked], "ctx", split_axis=0, concat_axis=0, tiled=True))

    width = w_out.shape[1] // groups
    w_rel = []
    for shift in range(groups):
        part = lax.dynamic_slice_in_dim(w_out, (group + shift) % groups * width, width, 1)
        w_rel.append(shifted(part, shift) if shift else part)
    mine = [group, group - 2, group + 2, group + 4]
    place = jnp.stack([g % groups for g in mine + [(g % groups) ^ 1 for g in mine]])
    w_cols = jnp.stack(w_rel)[(group - place) % groups].reshape(groups, heads_here, HD, width)
    w_heads = [w_cols[:, head].reshape(groups * HD, width) for head in range(heads_here)]

    live, w_heads = lax.optimization_barrier((live, w_heads))
    part = None
    for head in range(heads_here):
        attended = attend(head, slots, live, queries, kb, vb, incoming[head])
        part = project(gathered_pieces(attended), w_heads[head], part)
        if head == 0:
            live, part = lax.optimization_barrier((live, part))
    return part


def solution(mesh):
    in_specs = (
        P("ctx", "head"),
        P("ctx", "head"),
        P("ctx", "head"),
        P("ctx", None),
        P("head", None),
    )
    out_specs = P("ctx", "head")
    return jax.shard_map(
        on_device, mesh=mesh, in_specs=in_specs, out_specs=out_specs, check_vma=False
    )
```

```python
import functools

import jax
import jax.numpy as jnp
from jax import lax
from jax.experimental import pallas as pl
from jax.experimental.pallas import tpu as pltpu
from jax.sharding import PartitionSpec as P

HD = 128
BLK = 256
VMEM = 16 * 1024 * 1024
SCALE = HD ** (-0.5) * 1.4426950408889634


def fill_pools(jobs, sems):
    copies = [pltpu.make_async_copy(x, y, sems.at[i]) for i, (x, y) in enumerate(jobs)]
    for copy in copies:
        copy.start()
    for copy in copies:
        copy.wait()


def ones_beside(vpool):
    def fill(i, carry):
        vpool[i, :, pl.ds(HD, HD)] = jnp.ones((BLK, HD), jnp.bfloat16)
        return carry

    lax.fori_loop(0, vpool.shape[0], fill, 0)


def unpack_twice(packed, vpool):
    def fill(i, carry):
        x = packed[i]
        low, high = x[:, : HD // 2], x[:, HD // 2 :]
        vpool[i, pl.ds(0, BLK // 2), pl.ds(0, HD)] = jnp.concatenate([low, low], axis=1)
        vpool[i, pl.ds(BLK // 2, BLK // 2), pl.ds(0, HD)] = jnp.concatenate([high, high], axis=1)
        return carry

    lax.fori_loop(0, packed.shape[0], fill, 0)


def weights_of(block, q, kpool, slot_ref, live_ref):
    nt = (((1,), (1,)), ((), ()))
    rows = lax.broadcasted_iota(jnp.int32, (BLK, BLK), 0)
    keys = lax.broadcasted_iota(jnp.int32, (BLK, BLK), 1)
    slots = [block] + [slot_ref[block, p] for p in range(3)]
    scores = [lax.dot_general(q, kpool[s], nt, preferred_element_type=jnp.float32) for s in slots]
    scores[0] = jnp.where(keys <= rows, scores[0], -jnp.inf)
    for p in range(3):
        scores[p + 1] = scores[p + 1] + jnp.where(live_ref[block, p] != 0, 0.0, -jnp.inf)
    top = jnp.maximum(jnp.maximum(scores[0], scores[1]), jnp.maximum(scores[2], scores[3]))
    top = jnp.max(top, axis=1, keepdims=True) * SCALE
    return slots, [jnp.exp2(sc * SCALE - top).astype(jnp.bfloat16) for sc in scores]


def times_values(slots, weights, vpool):
    total = None
    for s, w in zip(slots, weights):
        term = jnp.dot(w, vpool[s], preferred_element_type=jnp.float32)
        total = term if total is None else total + term
    return total


def attend_kernel(slot_ref, live_ref, q_ref, here, come, o_ref, kpool, vpool, sems):
    j = pl.program_id(0)
    n, peers = here.shape[0], come.shape[0]
    near, far = pl.ds(0, n), pl.ds(n, peers)

    @pl.when(j == 0)
    def _():
        k_rows, v_rows = pl.ds(0, BLK), pl.ds(BLK, BLK)
        ones_beside(vpool)
        fill_pools(
            [
                (here.at[:, k_rows], kpool.at[near]),
                (come.at[:, k_rows], kpool.at[far]),
                (here.at[:, v_rows], vpool.at[near, :, pl.ds(0, HD)]),
                (come.at[:, v_rows], vpool.at[far, :, pl.ds(0, HD)]),
            ],
            sems,
        )

    for u in range(2):
        at = pl.ds(u * BLK, BLK)
        slots, weights = weights_of(2 * j + u, q_ref[at, :], kpool, slot_ref, live_ref)
        total = times_values(slots, weights, vpool)
        o_ref[at, :] = (total[:, :HD] / total[:, HD:]).astype(jnp.bfloat16)


def attend_first_kernel(
    slot_ref, live_ref, q_lo, q_hi, here, come, o_ref, w_lo, w_hi, r_lo, r_hi, kpool, vpool, packed, sems
):
    j = pl.program_id(0)
    n, peers = here.shape[0], come.shape[0]
    near, far = pl.ds(0, n), pl.ds(n, peers)

    @pl.when(j == 0)
    def _():
        k_rows, v_rows = pl.ds(2 * BLK, BLK), pl.ds(3 * BLK, BLK // 2)
        ones_beside(vpool)
        fill_pools(
            [
                (here.at[:, k_rows], kpool.at[near]),
                (come.at[:, k_rows], kpool.at[far]),
                (here.at[:, v_rows], packed.at[near]),
                (come.at[:, v_rows], packed.at[far]),
            ],
            sems,
        )
        unpack_twice(packed, vpool)

    out = []
    for block, q_ref, w_ref, r_ref in ((j, q_lo, w_lo, r_lo), (j + n // 2, q_hi, w_hi, r_hi)):
        slots, weights = weights_of(block, q_ref[...], kpool, slot_ref, live_ref)
        for i, w in enumerate(weights):
            w_ref[:, pl.ds(i * BLK, BLK)] = w
        total = times_values(slots, weights, vpool)
        r_ref[...] = 1.0 / total[:, HD:]
        out.append((total[:, :HD] / total[:, HD:]).astype(jnp.bfloat16))
    lanes = lax.broadcasted_iota(jnp.int32, (BLK, HD), 1)
    o_ref[...] = jnp.where(lanes < HD // 2, out[0], out[1])


def attend_last_kernel(slot_ref, here, come, w_lo, w_hi, r_lo, r_hi, o_ref, vpool, packed, sems):
    j = pl.program_id(0)
    n, peers = here.shape[0], come.shape[0]

    @pl.when(j == 0)
    def _():
        fill_pools([(here, packed.at[pl.ds(0, n)]), (come, packed.at[pl.ds(n, peers)])], sems)
        unpack_twice(packed, vpool)

    out = []
    for block, w_ref, r_ref in ((j, w_lo, r_lo), (j + n // 2, w_hi, r_hi)):
        slots = [block] + [slot_ref[block, p] for p in range(3)]
        total = times_values(slots, [w_ref[:, pl.ds(i * BLK, BLK)] for i in range(4)], vpool)
        out.append((total * r_ref[...]).astype(jnp.bfloat16))
    lanes = lax.broadcasted_iota(jnp.int32, (BLK, HD), 1)
    o_ref[...] = jnp.where(lanes < HD // 2, out[0], out[1])


def attend_call(kernel, scalars, first, whole, last, outs, scratch, steps, flops):
    return pl.pallas_call(
        kernel,
        out_shape=[pltpu.HBM(shape, dtype) if i else jax.ShapeDtypeStruct(shape, dtype) for i, (shape, dtype) in enumerate(outs)],
        grid_spec=pltpu.PrefetchScalarGridSpec(
            num_scalar_prefetch=len(scalars),
            grid=(steps,),
            in_specs=[pl.BlockSpec(shape, index) for _, shape, index in first]
            + [pl.BlockSpec(memory_space=pl.ANY) for _ in whole]
            + [pl.BlockSpec(shape, index) for _, shape, index in last],
            out_specs=[pl.BlockSpec((shape[0] // steps, shape[1]), lambda j, *_: (j, 0)) for shape, _ in outs],
            scratch_shapes=scratch + [pltpu.SemaphoreType.DMA((4,))],
        ),
        compiler_params=pltpu.CompilerParams(vmem_limit_bytes=VMEM),
        cost_estimate=pl.CostEstimate(flops=flops, bytes_accessed=8 * 1024 * 1024, transcendentals=flops // 512),
    )(*scalars, *[x for x, _, _ in first], *whole, *[x for x, _, _ in last])


def attend(head, slots, live, queries, here, come):
    rows = queries.shape[0]
    n = rows // BLK
    steps, pool = n // 2, n + come.shape[0]
    half = rows // 2
    scratch = [pltpu.VMEM((pool, BLK, HD), jnp.bfloat16), pltpu.VMEM((pool, BLK, 2 * HD), jnp.bfloat16)]
    flops = 16 * rows * BLK * HD
    if head == 0:
        first = [(queries, (2 * BLK, HD), lambda j, *_: (j, 0))]
        outs = [((rows, HD), jnp.bfloat16)]
        return attend_call(attend_kernel, (slots, live), first, (here, come), [], outs, scratch, steps, flops)
    first = [
        (queries, (BLK, HD), lambda j, *_: (j, 1)),
        (queries, (BLK, HD), lambda j, *_: (j + steps, 1)),
    ]
    outs = [((half, HD), jnp.bfloat16)] + [((half, 4 * BLK), jnp.bfloat16)] * 2 + [((half, HD), jnp.float32)] * 2
    scratch.append(pltpu.VMEM((pool, BLK // 2, HD), jnp.bfloat16))
    return attend_call(attend_first_kernel, (slots, live), first, (here, come), [], outs, scratch, steps, flops)


def attend_last(slots, here, come, w_lo, w_hi, r_lo, r_hi):
    half = w_lo.shape[0]
    n = here.shape[0]
    steps, pool = n // 2, n + come.shape[0]
    last = [(pltpu.with_memory_space_constraint(x, pltpu.HBM), (BLK, x.shape[1]), lambda j, *_: (j, 0)) for x in (w_lo, w_hi, r_lo, r_hi)]
    scratch = [pltpu.VMEM((pool, BLK, HD), jnp.bfloat16), pltpu.VMEM((pool, BLK // 2, HD), jnp.bfloat16)]
    outs = [((half, HD), jnp.bfloat16)]
    return attend_call(
        attend_last_kernel, (slots,), [], (here, come), last, outs, scratch, steps, 8 * half * BLK * HD
    )[0]


def shifted(x, shift):
    n = lax.axis_size("head")
    return lax.ppermute(x, "head", [(i, (i + shift) % n) for i in range(n)])


def swapped(x):
    return lax.ppermute(x, "head", [(i, i ^ 1) for i in range(lax.axis_size("head"))])


def gathered_pieces(own, beside=None):
    half = own.shape[0] // 2
    before, behind = shifted(own, 2), shifted(own, -2)
    if beside is not None:
        before, behind, beside = lax.optimization_barrier((before, behind, beside))
    own_s = swapped(own)
    top, bottom = shifted(before[:half], 2), shifted(behind[half:], -2)
    before_s, behind_s = swapped(before), swapped(behind)
    top_s, bottom_s = swapped(top), swapped(bottom)
    return [own, before, behind, top, bottom, own_s, before_s, behind_s, top_s, bottom_s], beside


def project_kernel(tile, *refs):
    pieces, w_ref, rest = refs[:10], refs[10], refs[11:]
    per = pieces[0].shape[0] // tile
    step = pl.program_id(0) % per
    first = step < per // 2
    at = pl.ds(pl.multiple_of(step * tile, tile), tile)
    at_half = pl.ds(pl.multiple_of(step % (per // 2) * tile, tile), tile)
    ordered = []
    for i in (0, 5):
        a0, a1, a2, top, bottom = pieces[i : i + 5]
        far = jnp.where(first, top[at_half, :], bottom[at_half, :])
        ordered += [a0[at, :], a1[at, :], a2[at, :], far]
    w = w_ref[pl.program_id(0) // per]
    out = jnp.dot(jnp.concatenate(ordered, axis=1), w, preferred_element_type=jnp.float32)
    if len(rest) == 2:
        out = out + rest[0][...]
    rest[-1][...] = out.astype(rest[-1].dtype)


def project(pieces, w, part, dtype):
    rows, width = pieces[0].shape[0] * w.shape[0], w.shape[-1]
    tile = rows // 4
    steps = rows // tile
    wide = pl.BlockSpec((tile, width), lambda i: (i, 0))
    more = [] if part is None else [part]
    return pl.pallas_call(
        functools.partial(project_kernel, tile),
        out_shape=jax.ShapeDtypeStruct((rows, width), dtype),
        grid=(steps,),
        in_specs=[pl.BlockSpec(memory_space=pltpu.VMEM)] * 11 + [wide] * len(more),
        out_specs=wide,
        compiler_params=pltpu.CompilerParams(vmem_limit_bytes=VMEM),
        cost_estimate=pl.CostEstimate(
            flops=2 * rows * w.shape[-2] * width, bytes_accessed=rows * 6 * width, transcendentals=0
        ),
    )(*pieces, w, *more)


def on_device(queries, keys, values, chosen, w_out):
    row_count, feature_width = queries.shape
    blocks_here = row_count // BLK
    heads_here = feature_width // HD
    device_count = lax.axis_size("ctx")
    my_index = lax.axis_index("ctx")
    groups = lax.axis_size("head")
    group = lax.axis_index("head")

    spread = jnp.broadcast_to(chosen[None], (device_count,) + chosen.shape)
    table = lax.all_to_all(spread, "ctx", split_axis=0, concat_axis=0, tiled=True)
    asked = jnp.max(jnp.where(table // blocks_here == my_index, table % blocks_here, 0), axis=(1, 2))

    owner_dev = chosen // blocks_here
    own_block = my_index * blocks_here + jnp.arange(blocks_here, dtype=jnp.int32)[:, None]
    live = (chosen != own_block).astype(jnp.int32)
    slots = jnp.where(owner_dev == my_index, chosen % blocks_here, blocks_here + owner_dev)

    def blocks(x, head):
        return x[:, head * HD : (head + 1) * HD].reshape(blocks_here, BLK, HD)

    def folded(x):
        return jnp.concatenate([x[:, : BLK // 2], x[:, BLK // 2 :]], axis=2)

    v1 = blocks(values, 1)
    here = jnp.concatenate(
        [blocks(keys, 0), blocks(values, 0), blocks(keys, 1), folded(v1[:, :, : HD // 2])], axis=1
    )
    here_last = folded(v1[:, :, HD // 2 :])
    come = lax.all_to_all(here[asked], "ctx", split_axis=0, concat_axis=0, tiled=True)

    width = w_out.shape[1] // groups
    w_rel = []
    for shift in range(groups):
        part = lax.dynamic_slice_in_dim(w_out, (group + shift) % groups * width, width, 1)
        w_rel.append(shifted(part, shift) if shift else part)
    mine = [group, group - 2, group + 2, group + 4]
    place = jnp.stack([g % groups for g in mine + [(g % groups) ^ 1 for g in mine]])
    w_cols = jnp.stack(w_rel)[(group - place) % groups].reshape(groups, heads_here, HD, width)
    w_first = w_cols[:, 0].reshape(1, groups * HD, width)
    w_pads = []
    for part in (w_cols[:, 1, : HD // 2], w_cols[:, 1, HD // 2 :]):
        empty = jnp.zeros_like(part)
        w_pads.append(
            jnp.stack([jnp.concatenate(x, axis=1).reshape(groups * HD, width) for x in ((part, empty), (empty, part))])
        )
    send_last, w_first, w_pads = lax.optimization_barrier((here_last[asked], w_first, w_pads))
    come_last = lax.all_to_all(send_last, "ctx", split_axis=0, concat_axis=0, tiled=True)

    attended = attend(0, slots, live, queries, here, come)[0]
    live, _ = lax.optimization_barrier((live, attended))
    packed, *rest = attend(1, slots, live, queries, here, come)
    pieces, packed = gathered_pieces(attended, packed)
    total = project(pieces, w_first, None, jnp.float32)
    pieces, _ = gathered_pieces(packed)
    total = project(pieces, w_pads[0], total, jnp.float32)
    packed = attend_last(slots, here_last, come_last, *rest)
    pieces, total = gathered_pieces(packed, total)
    return project(pieces, w_pads[1], total, jnp.bfloat16)


def solution(mesh):
    in_specs = (
        P("ctx", "head"),
        P("ctx", "head"),
        P("ctx", "head"),
        P("ctx", None),
        P("head", None),
    )
    out_specs = P("ctx", "head")
    return jax.shard_map(
        on_device, mesh=mesh, in_specs=in_specs, out_specs=out_specs, check_vma=False
    )
```

```python
import functools

import jax
import jax.numpy as jnp
from jax import lax
from jax.experimental import pallas as pl
from jax.experimental.pallas import tpu as pltpu
from jax.sharding import PartitionSpec as P

HD = 128
BLK = 256
VMEM = 16 * 1024 * 1024
SCALE = HD ** (-0.5) * 1.4426950408889634


def fill_pools(jobs, sems):
    copies = [pltpu.make_async_copy(x, y, sems.at[i]) for i, (x, y) in enumerate(jobs)]
    for copy in copies:
        copy.start()
    for copy in copies:
        copy.wait()


def ones_beside(vpool):
    def fill(i, carry):
        vpool[i, :, pl.ds(HD, HD)] = jnp.ones((BLK, HD), jnp.bfloat16)
        return carry

    lax.fori_loop(0, vpool.shape[0], fill, 0)


def weights_of(block, q, kpool, slot_ref, live_ref):
    nt = (((1,), (1,)), ((), ()))
    rows = lax.broadcasted_iota(jnp.int32, (BLK, BLK), 0)
    keys = lax.broadcasted_iota(jnp.int32, (BLK, BLK), 1)
    slots = [block] + [slot_ref[block, p] for p in range(3)]
    scores = [lax.dot_general(q, kpool[s], nt, preferred_element_type=jnp.float32) for s in slots]
    scores[0] = jnp.where(keys <= rows, scores[0], -jnp.inf)
    for p in range(3):
        scores[p + 1] = scores[p + 1] + jnp.where(live_ref[block, p] != 0, 0.0, -jnp.inf)
    top = jnp.maximum(jnp.maximum(scores[0], scores[1]), jnp.maximum(scores[2], scores[3]))
    top = jnp.max(top, axis=1, keepdims=True) * SCALE
    return slots, [jnp.exp2(sc * SCALE - top).astype(jnp.bfloat16) for sc in scores]


def times_values(slots, weights, vpool):
    total = None
    for s, w in zip(slots, weights):
        term = jnp.dot(w, vpool[s], preferred_element_type=jnp.float32)
        total = term if total is None else total + term
    return total


def attend_kernel(slot_ref, live_ref, q_ref, here, come, o_ref, kpool, vpool, sems):
    j = pl.program_id(0)
    n, peers = here.shape[0], come.shape[0]
    near, far = pl.ds(0, n), pl.ds(n, peers)

    @pl.when(j == 0)
    def _():
        k_rows, v_rows = pl.ds(0, BLK), pl.ds(BLK, BLK)
        ones_beside(vpool)
        fill_pools(
            [
                (here.at[:, k_rows], kpool.at[near]),
                (come.at[:, k_rows], kpool.at[far]),
                (here.at[:, v_rows], vpool.at[near, :, pl.ds(0, HD)]),
                (come.at[:, v_rows], vpool.at[far, :, pl.ds(0, HD)]),
            ],
            sems,
        )

    for u in range(2):
        at = pl.ds(u * BLK, BLK)
        slots, weights = weights_of(2 * j + u, q_ref[at, :], kpool, slot_ref, live_ref)
        total = times_values(slots, weights, vpool)
        o_ref[at, :] = (total[:, :HD] / total[:, HD:]).astype(jnp.bfloat16)


def attend_first_kernel(slot_ref, live_ref, q_ref, here, come, w_ref, r_ref, kpool, sems):
    j = pl.program_id(0)
    n, peers = here.shape[0], come.shape[0]

    @pl.when(j == 0)
    def _():
        rows = pl.ds(2 * BLK, BLK)
        fill_pools(
            [(here.at[:, rows], kpool.at[pl.ds(0, n)]), (come.at[:, rows], kpool.at[pl.ds(n, peers)])], sems
        )

    for u in range(2):
        at = pl.ds(u * BLK, BLK)
        _, weights = weights_of(2 * j + u, q_ref[at, :], kpool, slot_ref, live_ref)
        total = None
        for i, w in enumerate(weights):
            w_ref[at, pl.ds(i * BLK, BLK)] = w
            term = jnp.dot(w, jnp.ones((BLK, HD), jnp.bfloat16), preferred_element_type=jnp.float32)
            total = term if total is None else total + term
        r_ref[at, :] = 1.0 / total


def attend_last_kernel(slot_ref, here, come, w_ref, r_ref, o_ref, vpool, sems):
    j = pl.program_id(0)
    n, peers = here.shape[0], come.shape[0]

    @pl.when(j == 0)
    def _():
        fill_pools([(here, vpool.at[pl.ds(0, n)]), (come, vpool.at[pl.ds(n, peers)])], sems)

    for u in range(2):
        at = pl.ds(u * BLK, BLK)
        block = 2 * j + u
        slots = [block] + [slot_ref[block, p] for p in range(3)]
        total = times_values(slots, [w_ref[at, pl.ds(i * BLK, BLK)] for i in range(4)], vpool)
        o_ref[at, :] = (total * r_ref[at, :]).astype(jnp.bfloat16)


def attend_call(kernel, scalars, first, whole, last, outs, scratch, steps, flops):
    return pl.pallas_call(
        kernel,
        out_shape=[jax.ShapeDtypeStruct(*outs[0])] if len(outs) == 1 else [pltpu.HBM(*out) for out in outs],
        grid_spec=pltpu.PrefetchScalarGridSpec(
            num_scalar_prefetch=len(scalars),
            grid=(steps,),
            in_specs=[pl.BlockSpec(shape, index) for _, shape, index in first]
            + [pl.BlockSpec(memory_space=pl.ANY) for _ in whole]
            + [pl.BlockSpec(shape, index) for _, shape, index in last],
            out_specs=[pl.BlockSpec((shape[0] // steps, shape[1]), lambda j, *_: (j, 0)) for shape, _ in outs],
            scratch_shapes=scratch + [pltpu.SemaphoreType.DMA((4,))],
        ),
        compiler_params=pltpu.CompilerParams(vmem_limit_bytes=VMEM),
        cost_estimate=pl.CostEstimate(flops=flops, bytes_accessed=8 * 1024 * 1024, transcendentals=flops // 512),
    )(*scalars, *[x for x, _, _ in first], *whole, *[x for x, _, _ in last])


def attend(head, slots, live, queries, here, come):
    rows = queries.shape[0]
    n = rows // BLK
    steps, pool = n // 2, n + come.shape[0]
    first = [(queries, (2 * BLK, HD), lambda j, *_: (j, head))]
    kpool, vpool = pltpu.VMEM((pool, BLK, HD), jnp.bfloat16), pltpu.VMEM((pool, BLK, 2 * HD), jnp.bfloat16)
    flops = 16 * rows * BLK * HD
    if head == 0:
        kernel, outs, scratch = attend_kernel, [((rows, HD), jnp.bfloat16)], [kpool, vpool]
    else:
        outs = [((rows, 4 * BLK), jnp.bfloat16), ((rows, HD), jnp.float32)]
        kernel, scratch = attend_first_kernel, [kpool]
    return attend_call(kernel, (slots, live), first, (here, come), [], outs, scratch, steps, flops)


def attend_last(slots, here, come, *weights):
    rows = weights[0].shape[0]
    n = here.shape[0]
    steps, pool = n // 2, n + come.shape[0]
    last = [(pltpu.with_memory_space_constraint(x, pltpu.HBM), (2 * BLK, x.shape[1]), lambda j, *_: (j, 0)) for x in weights]
    outs = [((rows, HD), jnp.bfloat16)]
    scratch = [pltpu.VMEM((pool, BLK, HD), jnp.bfloat16)]
    return attend_call(
        attend_last_kernel, (slots,), [], (here, come), last, outs, scratch, steps, 8 * rows * BLK * HD
    )[0]


def shifted(x, shift):
    n = lax.axis_size("head")
    return lax.ppermute(x, "head", [(i, (i + shift) % n) for i in range(n)])


def swapped(x):
    return lax.ppermute(x, "head", [(i, i ^ 1) for i in range(lax.axis_size("head"))])


def gather_and_project(own, w_near, w_far, total, dtype):
    half = own.shape[0] // 2
    before, behind = shifted(own, 2), shifted(own, -2)
    far = [shifted(before[:half], 2), shifted(behind[half:], -2)]
    near = [own, before, behind]
    total = project(True, near + [swapped(x) for x in near], w_near, total, jnp.float32)
    far, total = lax.optimization_barrier((far, total))
    return project(False, far + [swapped(x) for x in far], w_far, total, dtype)


def project_kernel(tile, near, count, *refs):
    pieces, w_ref, rest = refs[:count], refs[count], refs[count + 1 :]
    step, half = pl.program_id(0), pl.num_programs(0) // 2
    at = pl.ds(pl.multiple_of(step * tile, tile), tile)
    at_half = pl.ds(pl.multiple_of(step % half * tile, tile), tile)
    if near:
        ordered = [x[at, :] for x in pieces]
    else:
        ordered = [
            jnp.where(step < half, pieces[i][at_half, :], pieces[i + 1][at_half, :]) for i in range(0, count, 2)
        ]
    out = jnp.dot(jnp.concatenate(ordered, axis=1), w_ref[...], preferred_element_type=jnp.float32)
    if len(rest) == 2:
        out = out + rest[0][...]
    rest[-1][...] = out.astype(rest[-1].dtype)


def project(near, pieces, w, part, dtype):
    rows, width = pieces[0].shape[0] * (1 if near else 2), w.shape[-1]
    steps = 4
    tile = rows // steps
    wide = pl.BlockSpec((tile, width), lambda i: (i, 0))
    more = [] if part is None else [part]
    return pl.pallas_call(
        functools.partial(project_kernel, tile, near, len(pieces)),
        out_shape=jax.ShapeDtypeStruct((rows, width), dtype),
        grid=(steps,),
        in_specs=[pl.BlockSpec(memory_space=pltpu.VMEM)] * (len(pieces) + 1) + [wide] * len(more),
        out_specs=wide,
        compiler_params=pltpu.CompilerParams(vmem_limit_bytes=VMEM),
        cost_estimate=pl.CostEstimate(
            flops=2 * rows * w.shape[0] * width, bytes_accessed=rows * 6 * width, transcendentals=0
        ),
    )(*pieces, w, *more)


def on_device(queries, keys, values, chosen, w_out):
    row_count, feature_width = queries.shape
    blocks_here = row_count // BLK
    heads_here = feature_width // HD
    device_count = lax.axis_size("ctx")
    my_index = lax.axis_index("ctx")
    groups = lax.axis_size("head")
    group = lax.axis_index("head")

    spread = jnp.broadcast_to(chosen[None], (device_count,) + chosen.shape)
    table = lax.all_to_all(spread, "ctx", split_axis=0, concat_axis=0, tiled=True)
    asked = jnp.max(jnp.where(table // blocks_here == my_index, table % blocks_here, 0), axis=(1, 2))

    owner_dev = chosen // blocks_here
    own_block = my_index * blocks_here + jnp.arange(blocks_here, dtype=jnp.int32)[:, None]
    live = (chosen != own_block).astype(jnp.int32)
    slots = jnp.where(owner_dev == my_index, chosen % blocks_here, blocks_here + owner_dev)

    def blocks(x, head):
        return x[:, head * HD : (head + 1) * HD].reshape(blocks_here, BLK, HD)

    here = jnp.concatenate([blocks(keys, 0), blocks(values, 0), blocks(keys, 1)], axis=1)
    here_last = blocks(values, 1)
    come = lax.all_to_all(here[asked], "ctx", split_axis=0, concat_axis=0, tiled=True)

    width = w_out.shape[1] // groups
    w_rel = []
    for shift in range(groups):
        part = lax.dynamic_slice_in_dim(w_out, (group + shift) % groups * width, width, 1)
        w_rel.append(shifted(part, shift) if shift else part)
    mine = [group, group - 2, group + 2]
    places = [x % groups for x in mine + [x ^ 1 for x in mine]], [(group + 4) % groups, (group + 4) % groups ^ 1]
    w_rel = jnp.stack(w_rel).reshape(groups, heads_here, HD, width)
    w_near, w_far = [w_rel[(group - jnp.stack(place)) % groups] for place in places]
    w_near, w_far = [[w[:, head].reshape(-1, width) for head in range(heads_here)] for w in (w_near, w_far)]
    send_last, w_near, w_far = lax.optimization_barrier((here_last[asked], w_near, w_far))
    come_last = lax.all_to_all(send_last, "ctx", split_axis=0, concat_axis=0, tiled=True)

    attended = attend(0, slots, live, queries, here, come)[0]
    live, _ = lax.optimization_barrier((live, attended))
    weights = attend(1, slots, live, queries, here, come)
    total = gather_and_project(attended, w_near[0], w_far[0], None, jnp.float32)
    slots, total = lax.optimization_barrier((slots, total))
    attended = attend_last(slots, here_last, come_last, *weights)
    return gather_and_project(attended, w_near[1], w_far[1], total, jnp.bfloat16)


def solution(mesh):
    in_specs = (
        P("ctx", "head"),
        P("ctx", "head"),
        P("ctx", "head"),
        P("ctx", None),
        P("head", None),
    )
    out_specs = P("ctx", "head")
    return jax.shard_map(
        on_device, mesh=mesh, in_specs=in_specs, out_specs=out_specs, check_vma=False
    )
```

```python
import functools

import jax
import jax.numpy as jnp
from jax import lax
from jax.experimental import pallas as pl
from jax.experimental.pallas import tpu as pltpu
from jax.sharding import PartitionSpec as P

HD = 128
BLK = 256
VMEM = 18 * 1024 * 1024
SCALE = HD ** (-0.5) * 1.4426950408889634


def attend_kernel(head, blocks_here, blocks, slot_ref, live_ref, q_ref, k_hbm, v_hbm, in_hbm, o_ref, kpool, vpool, sems):
    peers = in_hbm.shape[0]
    cols, lanes = pl.ds(head * HD, HD), pl.ds(0, HD)
    near, far = pl.ds(0, blocks_here), pl.ds(blocks_here, peers)
    copies = [
        pltpu.make_async_copy(k_hbm.at[:, :, cols], kpool.at[near], sems.at[0]),
        pltpu.make_async_copy(in_hbm.at[:, 0], kpool.at[far], sems.at[1]),
        pltpu.make_async_copy(v_hbm.at[:, :, cols], vpool.at[near, :, lanes], sems.at[2]),
        pltpu.make_async_copy(in_hbm.at[:, 1], vpool.at[far, :, lanes], sems.at[3]),
    ]
    for copy in copies:
        copy.start()

    def fill(i, carry):
        vpool[i, :, pl.ds(HD, HD)] = jnp.ones((BLK, HD), jnp.bfloat16)
        return carry

    lax.fori_loop(0, blocks_here + peers, fill, 0)
    for copy in copies:
        copy.wait()

    nt = (((1,), (1,)), ((), ()))
    rows = lax.broadcasted_iota(jnp.int32, (BLK, BLK), 0)
    keys = lax.broadcasted_iota(jnp.int32, (BLK, BLK), 1)
    for i, block in enumerate(blocks):
        at = pl.ds(i * BLK, BLK)
        q = q_ref[at, :]
        slots = [block] + [slot_ref[block, p] for p in range(3)]
        scores = [lax.dot_general(q, kpool[s], nt, preferred_element_type=jnp.float32) for s in slots]
        scores[0] = jnp.where(keys <= rows, scores[0], -jnp.inf)
        for p in range(3):
            scores[p + 1] = scores[p + 1] + jnp.where(live_ref[block, p] != 0, 0.0, -jnp.inf)
        top = jnp.maximum(jnp.maximum(scores[0], scores[1]), jnp.maximum(scores[2], scores[3]))
        top = jnp.max(top, axis=1, keepdims=True) * SCALE
        total = None
        for s, sc in zip(slots, scores):
            w = jnp.exp2(sc * SCALE - top).astype(jnp.bfloat16)
            term = jnp.dot(w, vpool[s], preferred_element_type=jnp.float32)
            total = term if total is None else total + term
        o_ref[at, :] = (total[:, :HD] / total[:, HD:]).astype(jnp.bfloat16)


def attend(head, parts, part, slots, live, queries, kb, vb, incoming):
    blocks_here = kb.shape[0]
    count = blocks_here // parts
    blocks = range(part * count, (part + 1) * count)
    rows = count * BLK
    pool = blocks_here + incoming.shape[0]
    return pl.pallas_call(
        functools.partial(attend_kernel, head, blocks_here, blocks),
        out_shape=jax.ShapeDtypeStruct((rows, HD), jnp.bfloat16),
        grid_spec=pltpu.PrefetchScalarGridSpec(
            num_scalar_prefetch=2,
            grid=(1,),
            in_specs=[pl.BlockSpec((rows, HD), lambda j, *_: (part, head))] + [pl.BlockSpec(memory_space=pl.ANY)] * 3,
            out_specs=pl.BlockSpec((rows, HD), lambda j, *_: (0, 0)),
            scratch_shapes=[
                pltpu.VMEM((pool, BLK, HD), jnp.bfloat16),
                pltpu.VMEM((pool, BLK, 2 * HD), jnp.bfloat16),
                pltpu.SemaphoreType.DMA((4,)),
            ],
        ),
        compiler_params=pltpu.CompilerParams(vmem_limit_bytes=VMEM),
        cost_estimate=pl.CostEstimate(
            flops=4 * rows * 4 * BLK * HD, bytes_accessed=pool * BLK * HD * 4, transcendentals=rows * 4 * BLK
        ),
    )(slots, live, queries, kb, vb, incoming)


def shifted(x, shift):
    n = lax.axis_size("head")
    return lax.ppermute(x, "head", [(i, (i + shift) % n) for i in range(n)])


def swapped(x):
    return lax.ppermute(x, "head", [(i, i ^ 1) for i in range(lax.axis_size("head"))])


def gathered_pieces(own):
    half = own.shape[0] // 2
    before, behind = shifted(own, 2), shifted(own, -2)
    own_s = swapped(own)
    top, bottom = shifted(before[:half], 2), shifted(behind[half:], -2)
    before_s, behind_s = swapped(before), swapped(behind)
    top_s, bottom_s = swapped(top), swapped(bottom)
    return [own, before, behind, top, bottom, own_s, before_s, behind_s, top_s, bottom_s]


def project_kernel(tile, *refs):
    pieces, w_ref, rest = refs[:10], refs[10], refs[11:]
    step, steps = pl.program_id(0), pl.num_programs(0)
    first = step < steps // 2
    at = pl.ds(pl.multiple_of(step * tile, tile), tile)
    at_half = pl.ds(pl.multiple_of(step % (steps // 2) * tile, tile), tile)
    ordered = []
    for i in (0, 5):
        a0, a1, a2, top, bottom = pieces[i : i + 5]
        far = jnp.where(first, top[at_half, :], bottom[at_half, :])
        ordered += [a0[at, :], a1[at, :], a2[at, :], far]
    out = jnp.dot(jnp.concatenate(ordered, axis=1), w_ref[...], preferred_element_type=jnp.float32)
    if len(rest) > 1:
        out = out + rest[0][...]
    rest[-1][...] = out.astype(rest[-1].dtype)


def project(pieces, w, part, dtype, half=None, into=None):
    rows, width = pieces[0].shape[0], w.shape[1]
    steps = 4
    tile = rows // steps
    shift = 0 if half is None else half * steps
    wide = pl.BlockSpec((tile, width), lambda i: (i + shift, 0))
    more = [] if part is None else [part]
    held = [] if into is None else [into]
    return pl.pallas_call(
        functools.partial(project_kernel, tile),
        out_shape=jax.ShapeDtypeStruct((rows if half is None else 2 * rows, width), dtype),
        grid=(steps,),
        in_specs=[pl.BlockSpec(memory_space=pltpu.VMEM)] * 11
        + [wide] * len(more)
        + [pl.BlockSpec(memory_space=pl.ANY)] * len(held),
        out_specs=wide,
        input_output_aliases={12: 0} if held else {},
        compiler_params=pltpu.CompilerParams(vmem_limit_bytes=VMEM),
        cost_estimate=pl.CostEstimate(
            flops=2 * rows * w.shape[0] * width, bytes_accessed=rows * 6 * width, transcendentals=0
        ),
    )(*pieces, w, *more, *held)


def on_device(queries, keys, values, chosen, w_out):
    row_count, feature_width = queries.shape
    blocks_here = row_count // BLK
    heads_here = feature_width // HD
    device_count = lax.axis_size("ctx")
    my_index = lax.axis_index("ctx")
    groups = lax.axis_size("head")
    group = lax.axis_index("head")

    spread = jnp.broadcast_to(chosen[None], (device_count,) + chosen.shape)
    table = lax.all_to_all(spread, "ctx", split_axis=0, concat_axis=0, tiled=True)
    asked = jnp.max(jnp.where(table // blocks_here == my_index, table % blocks_here, 0), axis=(1, 2))

    owner_dev = chosen // blocks_here
    own_block = my_index * blocks_here + jnp.arange(blocks_here, dtype=jnp.int32)[:, None]
    live = (chosen != own_block).astype(jnp.int32)
    slots = jnp.where(owner_dev == my_index, chosen % blocks_here, blocks_here + owner_dev)

    kb = keys.reshape(blocks_here, BLK, feature_width)
    vb = values.reshape(blocks_here, BLK, feature_width)
    sends = []
    for head in range(heads_here):
        cols = slice(head * HD, (head + 1) * HD)
        sends.append(jnp.stack([kb[:, :, cols], vb[:, :, cols]], axis=1)[asked])

    width = w_out.shape[1] // groups
    w_rel = []
    for shift in range(groups):
        part = lax.dynamic_slice_in_dim(w_out, (group + shift) % groups * width, width, 1)
        w_rel.append(shifted(part, shift) if shift else part)
    mine = [group, group - 2, group + 2, group + 4]
    place = jnp.stack([g % groups for g in mine + [(g % groups) ^ 1 for g in mine]])
    w_rel = jnp.stack(w_rel).reshape(groups, heads_here, HD, width)
    w_cols = w_rel[(group - place) % groups]
    w_heads = [w_cols[:, head].reshape(groups * HD, width) for head in range(heads_here)]

    sends[1], w_heads = lax.optimization_barrier((sends[1], w_heads))
    incoming = [lax.all_to_all(x, "ctx", split_axis=0, concat_axis=0, tiled=True) for x in sends]
    attended = attend(0, 1, 0, slots, live, queries, kb, vb, incoming[0])
    total = project(gathered_pieces(attended), w_heads[0], None, jnp.float32)
    live, total = lax.optimization_barrier((live, total))
    low = attend(1, 2, 0, slots, live, queries, kb, vb, incoming[1])
    live, low = lax.optimization_barrier((live, low))
    high = attend(1, 2, 1, slots, live, queries, kb, vb, incoming[1])
    pieces = gathered_pieces(low)
    high, _ = lax.optimization_barrier((high, pieces[1:3]))
    out = project(pieces, w_heads[1], total, jnp.bfloat16, 0)
    return project(gathered_pieces(high), w_heads[1], total, jnp.bfloat16, 1, out)


def solution(mesh):
    in_specs = (
        P("ctx", "head"),
        P("ctx", "head"),
        P("ctx", "head"),
        P("ctx", None),
        P("head", None),
    )
    out_specs = P("ctx", "head")
    return jax.shard_map(
        on_device, mesh=mesh, in_specs=in_specs, out_specs=out_specs, check_vma=False
    )
```

```python
import functools

import jax
import jax.numpy as jnp
from jax import lax
from jax.experimental import pallas as pl
from jax.experimental.pallas import tpu as pltpu
from jax.sharding import PartitionSpec as P

HD = 128
BLK = 256
VMEM = 18 * 1024 * 1024
SCALE = HD ** (-0.5) * 1.4426950408889634


def attend_kernel(head, blocks_here, slot_ref, live_ref, q_ref, k_hbm, v_hbm, in_hbm, o_ref, kpool, vpool, sems):
    peers = in_hbm.shape[0]
    cols, lanes = pl.ds(head * HD, HD), pl.ds(0, HD)
    near, far = pl.ds(0, blocks_here), pl.ds(blocks_here, peers)
    copies = [
        pltpu.make_async_copy(k_hbm.at[:, :, cols], kpool.at[near], sems.at[0]),
        pltpu.make_async_copy(in_hbm.at[:, 0], kpool.at[far], sems.at[1]),
        pltpu.make_async_copy(v_hbm.at[:, :, cols], vpool.at[near, :, lanes], sems.at[2]),
        pltpu.make_async_copy(in_hbm.at[:, 1], vpool.at[far, :, lanes], sems.at[3]),
    ]
    for copy in copies:
        copy.start()

    def fill(i, carry):
        vpool[i, :, pl.ds(HD, HD)] = jnp.ones((BLK, HD), jnp.bfloat16)
        return carry

    lax.fori_loop(0, blocks_here + peers, fill, 0)
    for copy in copies[:2]:
        copy.wait()

    nt = (((1,), (1,)), ((), ()))
    rows = lax.broadcasted_iota(jnp.int32, (BLK, BLK), 0)
    keys = lax.broadcasted_iota(jnp.int32, (BLK, BLK), 1)
    for block in range(blocks_here):
        at = pl.ds(block * BLK, BLK)
        q = q_ref[at, :]
        slots = [block] + [slot_ref[block, p] for p in range(3)]
        scores = [lax.dot_general(q, kpool[s], nt, preferred_element_type=jnp.float32) for s in slots]
        scores[0] = jnp.where(keys <= rows, scores[0], -jnp.inf)
        for p in range(3):
            scores[p + 1] = scores[p + 1] + jnp.where(live_ref[block, p] != 0, 0.0, -jnp.inf)
        if block == 0:
            for copy in copies[2:]:
                copy.wait()
        top = jnp.maximum(jnp.maximum(scores[0], scores[1]), jnp.maximum(scores[2], scores[3]))
        top = jnp.max(top, axis=1, keepdims=True) * SCALE
        total = None
        for s, sc in zip(slots, scores):
            w = jnp.exp2(sc * SCALE - top).astype(jnp.bfloat16)
            term = jnp.dot(w, vpool[s], preferred_element_type=jnp.float32)
            total = term if total is None else total + term
        o_ref[at, :] = (total[:, :HD] / total[:, HD:]).astype(jnp.bfloat16)


def attend(head, slots, live, queries, kb, vb, incoming):
    rows = queries.shape[0]
    blocks_here = rows // BLK
    pool = blocks_here + incoming.shape[0]
    return pl.pallas_call(
        functools.partial(attend_kernel, head, blocks_here),
        out_shape=jax.ShapeDtypeStruct((rows, HD), jnp.bfloat16),
        grid_spec=pltpu.PrefetchScalarGridSpec(
            num_scalar_prefetch=2,
            grid=(1,),
            in_specs=[pl.BlockSpec((rows, HD), lambda j, *_: (0, head))] + [pl.BlockSpec(memory_space=pl.ANY)] * 3,
            out_specs=pl.BlockSpec((rows, HD), lambda j, *_: (0, 0)),
            scratch_shapes=[
                pltpu.VMEM((pool, BLK, HD), jnp.bfloat16),
                pltpu.VMEM((pool, BLK, 2 * HD), jnp.bfloat16),
                pltpu.SemaphoreType.DMA((4,)),
            ],
        ),
        compiler_params=pltpu.CompilerParams(vmem_limit_bytes=VMEM),
        cost_estimate=pl.CostEstimate(
            flops=4 * rows * 4 * BLK * HD, bytes_accessed=pool * BLK * HD * 4, transcendentals=rows * 4 * BLK
        ),
    )(slots, live, queries, kb, vb, incoming)


def shifted(x, shift):
    n = lax.axis_size("head")
    return lax.ppermute(x, "head", [(i, (i + shift) % n) for i in range(n)])


def swapped(x):
    return lax.ppermute(x, "head", [(i, i ^ 1) for i in range(lax.axis_size("head"))])


def gathered_pieces(own):
    half = own.shape[0] // 2
    before, behind = shifted(own, 2), shifted(own, -2)
    own_s = swapped(own)
    top, bottom = shifted(before[:half], 2), shifted(behind[half:], -2)
    before_s, behind_s = swapped(before), swapped(behind)
    top_s, bottom_s = swapped(top), swapped(bottom)
    return [own, before, behind, top, bottom, own_s, before_s, behind_s, top_s, bottom_s]


def project_kernel(tile, *refs):
    pieces, w_ref, rest = refs[:10], refs[10], refs[11:]
    step, steps = pl.program_id(0), pl.num_programs(0)
    first = step < steps // 2
    at = pl.ds(pl.multiple_of(step * tile, tile), tile)
    at_half = pl.ds(pl.multiple_of(step % (steps // 2) * tile, tile), tile)
    ordered = []
    for i in (0, 5):
        a0, a1, a2, top, bottom = pieces[i : i + 5]
        far = jnp.where(first, top[at_half, :], bottom[at_half, :])
        ordered += [a0[at, :], a1[at, :], a2[at, :], far]
    out = jnp.dot(jnp.concatenate(ordered, axis=1), w_ref[...], preferred_element_type=jnp.float32)
    if len(rest) > 1:
        out = out + rest[0][at, :]
    rest[-1][...] = out.astype(rest[-1].dtype)


def project(pieces, w, part, dtype):
    rows, width = pieces[0].shape[0], w.shape[1]
    steps = 4
    tile = rows // steps
    more = [] if part is None else [part]
    return pl.pallas_call(
        functools.partial(project_kernel, tile),
        out_shape=jax.ShapeDtypeStruct((rows, width), dtype),
        grid=(steps,),
        in_specs=[pl.BlockSpec(memory_space=pltpu.VMEM)] * (11 + len(more)),
        out_specs=pl.BlockSpec((tile, width), lambda i: (i, 0)),
        compiler_params=pltpu.CompilerParams(vmem_limit_bytes=VMEM),
        cost_estimate=pl.CostEstimate(
            flops=2 * rows * w.shape[0] * width, bytes_accessed=rows * 6 * width, transcendentals=0
        ),
    )(*pieces, w, *more)


def on_device(queries, keys, values, chosen, w_out):
    row_count, feature_width = queries.shape
    blocks_here = row_count // BLK
    heads_here = feature_width // HD
    device_count = lax.axis_size("ctx")
    my_index = lax.axis_index("ctx")
    groups = lax.axis_size("head")
    group = lax.axis_index("head")

    spread = jnp.broadcast_to(chosen[None], (device_count,) + chosen.shape)
    table = lax.all_to_all(spread, "ctx", split_axis=0, concat_axis=0, tiled=True)
    asked = jnp.max(jnp.where(table // blocks_here == my_index, table % blocks_here, 0), axis=(1, 2))

    owner_dev = chosen // blocks_here
    own_block = my_index * blocks_here + jnp.arange(blocks_here, dtype=jnp.int32)[:, None]
    live = (chosen != own_block).astype(jnp.int32)
    slots = jnp.where(owner_dev == my_index, chosen % blocks_here, blocks_here + owner_dev)

    kb = keys.reshape(blocks_here, BLK, feature_width)
    vb = values.reshape(blocks_here, BLK, feature_width)
    sends = []
    for head in range(heads_here):
        cols = slice(head * HD, (head + 1) * HD)
        sends.append(jnp.stack([kb[:, :, cols], vb[:, :, cols]], axis=1)[asked])

    width = w_out.shape[1] // groups
    w_rel = []
    for shift in range(groups):
        part = lax.dynamic_slice_in_dim(w_out, (group + shift) % groups * width, width, 1)
        w_rel.append(shifted(part, shift) if shift else part)
    mine = [group, group - 2, group + 2, group + 4]
    place = jnp.stack([g % groups for g in mine + [(g % groups) ^ 1 for g in mine]])
    w_rel = jnp.stack(w_rel).reshape(groups, heads_here, HD, width)
    w_cols = w_rel[(group - place) % groups]
    w_heads = [w_cols[:, head].reshape(groups * HD, width) for head in range(heads_here)]

    sends[1], w_heads = lax.optimization_barrier((sends[1], w_heads))
    incoming = [lax.all_to_all(x, "ctx", split_axis=0, concat_axis=0, tiled=True) for x in sends]
    part = None
    for head in range(heads_here):
        attended = attend(head, slots, live, queries, kb, vb, incoming[head])
        part = project(gathered_pieces(attended), w_heads[head], part, jnp.bfloat16 if head else jnp.float32)
        live, part = lax.optimization_barrier((live, part))
    return part


def solution(mesh):
    in_specs = (
        P("ctx", "head"),
        P("ctx", "head"),
        P("ctx", "head"),
        P("ctx", None),
        P("head", None),
    )
    out_specs = P("ctx", "head")
    return jax.shard_map(
        on_device, mesh=mesh, in_specs=in_specs, out_specs=out_specs, check_vma=False
    )
```

```python
import functools

import jax
import jax.numpy as jnp
from jax import lax
from jax.experimental import pallas as pl
from jax.experimental.pallas import tpu as pltpu
from jax.sharding import PartitionSpec as P

HD = 128
BLK = 256
VMEM = 18 * 1024 * 1024
SCALE = HD ** (-0.5) * 1.4426950408889634


def attend_kernel(head, blocks_here, slot_ref, live_ref, q_ref, k_hbm, v_hbm, in_hbm, o_ref, kpool, vpool, sems):
    peers = in_hbm.shape[0]
    cols, lanes = pl.ds(head * HD, HD), pl.ds(0, HD)
    near, far = pl.ds(0, blocks_here), pl.ds(blocks_here, peers)
    copies = [
        pltpu.make_async_copy(k_hbm.at[:, :, cols], kpool.at[near], sems.at[0]),
        pltpu.make_async_copy(in_hbm.at[:, 0], kpool.at[far], sems.at[1]),
        pltpu.make_async_copy(v_hbm.at[:, :, cols], vpool.at[near, :, lanes], sems.at[2]),
        pltpu.make_async_copy(in_hbm.at[:, 1], vpool.at[far, :, lanes], sems.at[3]),
    ]
    for copy in copies:
        copy.start()

    def fill(i, carry):
        vpool[i, :, pl.ds(HD, HD)] = jnp.ones((BLK, HD), jnp.bfloat16)
        return carry

    lax.fori_loop(0, blocks_here + peers, fill, 0)
    for copy in copies[:2]:
        copy.wait()

    nt = (((1,), (1,)), ((), ()))
    rows = lax.broadcasted_iota(jnp.int32, (BLK, BLK), 0)
    keys = lax.broadcasted_iota(jnp.int32, (BLK, BLK), 1)
    for block in range(blocks_here):
        at = pl.ds(block * BLK, BLK)
        q = q_ref[at, :]
        slots = [block] + [slot_ref[block, p] for p in range(3)]
        scores = [lax.dot_general(q, kpool[s], nt, preferred_element_type=jnp.float32) for s in slots]
        scores[0] = jnp.where(keys <= rows, scores[0], -jnp.inf)
        for p in range(3):
            scores[p + 1] = scores[p + 1] + jnp.where(live_ref[block, p] != 0, 0.0, -jnp.inf)
        if block == 0:
            for copy in copies[2:]:
                copy.wait()
        top = jnp.maximum(jnp.maximum(scores[0], scores[1]), jnp.maximum(scores[2], scores[3]))
        top = jnp.max(top, axis=1, keepdims=True) * SCALE
        total = None
        for s, sc in zip(slots, scores):
            w = jnp.exp2(sc * SCALE - top).astype(jnp.bfloat16)
            term = jnp.dot(w, vpool[s], preferred_element_type=jnp.float32)
            total = term if total is None else total + term
        o_ref[at, :] = (total[:, :HD] / total[:, HD:]).astype(jnp.bfloat16)


def attend(head, slots, live, queries, kb, vb, incoming):
    rows = queries.shape[0]
    blocks_here = rows // BLK
    pool = blocks_here + incoming.shape[0]
    return pl.pallas_call(
        functools.partial(attend_kernel, head, blocks_here),
        out_shape=jax.ShapeDtypeStruct((rows, HD), jnp.bfloat16),
        grid_spec=pltpu.PrefetchScalarGridSpec(
            num_scalar_prefetch=2,
            grid=(1,),
            in_specs=[pl.BlockSpec((rows, HD), lambda j, *_: (0, head))] + [pl.BlockSpec(memory_space=pl.ANY)] * 3,
            out_specs=pl.BlockSpec((rows, HD), lambda j, *_: (0, 0)),
            scratch_shapes=[
                pltpu.VMEM((pool, BLK, HD), jnp.bfloat16),
                pltpu.VMEM((pool, BLK, 2 * HD), jnp.bfloat16),
                pltpu.SemaphoreType.DMA((4,)),
            ],
        ),
        compiler_params=pltpu.CompilerParams(vmem_limit_bytes=VMEM),
        cost_estimate=pl.CostEstimate(
            flops=4 * rows * 4 * BLK * HD, bytes_accessed=pool * BLK * HD * 4, transcendentals=rows * 4 * BLK
        ),
    )(slots, live, queries, kb, vb, incoming)


def shifted(x, shift):
    n = lax.axis_size("head")
    return lax.ppermute(x, "head", [(i, (i + shift) % n) for i in range(n)])


def swapped(x):
    return lax.ppermute(x, "head", [(i, i ^ 1) for i in range(lax.axis_size("head"))])


def gathered_pieces(own):
    half = own.shape[0] // 2
    before, behind = shifted(own, 2), shifted(own, -2)
    own_s = swapped(own)
    top, bottom = shifted(before[:half], 2), shifted(behind[half:], -2)
    before_s, behind_s = swapped(before), swapped(behind)
    top_s, bottom_s = swapped(top), swapped(bottom)
    return [own, before, behind, top, bottom, own_s, before_s, behind_s, top_s, bottom_s]


def project_kernel(tile, *refs):
    pieces, w_ref, rest = refs[:10], refs[10], refs[11:]
    o_ref, buffer, sems = rest[-3:]
    rows = buffer.shape[0]
    copies = []
    for step in range(rows // tile):
        at = pl.ds(step * tile, tile)
        ordered = []
        for i in (0, 5):
            a0, a1, a2, top, bottom = pieces[i : i + 5]
            far = top if step * tile < rows // 2 else bottom
            ordered += [a0[at, :], a1[at, :], a2[at, :], far[pl.ds(step * tile % (rows // 2), tile), :]]
        out = jnp.dot(jnp.concatenate(ordered, axis=1), w_ref[...], preferred_element_type=jnp.float32)
        if len(rest) == 4:
            out = out + rest[0][at, :]
        buffer[at, :] = out.astype(buffer.dtype)
        copies.append(pltpu.make_async_copy(buffer.at[at], o_ref.at[at], sems.at[step]))
        copies[-1].start()
    for copy in copies:
        copy.wait()


def project(pieces, w, part, dtype):
    rows, width = pieces[0].shape[0], w.shape[1]
    steps = 8
    tile = rows // steps
    more = [] if part is None else [part]
    return pl.pallas_call(
        functools.partial(project_kernel, tile),
        out_shape=jax.ShapeDtypeStruct((rows, width), dtype),
        in_specs=[pl.BlockSpec(memory_space=pltpu.VMEM)] * (11 + len(more)),
        out_specs=pl.BlockSpec(memory_space=pl.ANY),
        scratch_shapes=[pltpu.VMEM((rows, width), dtype), pltpu.SemaphoreType.DMA((steps,))],
        compiler_params=pltpu.CompilerParams(vmem_limit_bytes=VMEM),
        cost_estimate=pl.CostEstimate(
            flops=2 * rows * w.shape[0] * width, bytes_accessed=rows * 6 * width, transcendentals=0
        ),
    )(*pieces, w, *more)


def on_device(queries, keys, values, chosen, w_out):
    row_count, feature_width = queries.shape
    blocks_here = row_count // BLK
    heads_here = feature_width // HD
    device_count = lax.axis_size("ctx")
    my_index = lax.axis_index("ctx")
    groups = lax.axis_size("head")
    group = lax.axis_index("head")

    spread = jnp.broadcast_to(chosen.T[None], (device_count,) + chosen.T.shape)
    table = lax.all_to_all(spread, "ctx", split_axis=0, concat_axis=0, tiled=True)
    asked = jnp.max(jnp.where(table // blocks_here == my_index, table % blocks_here, 0), axis=(1, 2))

    owner_dev = chosen // blocks_here
    own_block = my_index * blocks_here + jnp.arange(blocks_here, dtype=jnp.int32)[:, None]
    live = (chosen != own_block).astype(jnp.int32)
    slots = jnp.where(owner_dev == my_index, chosen % blocks_here, blocks_here + owner_dev)

    kb = keys.reshape(blocks_here, BLK, feature_width)
    vb = values.reshape(blocks_here, BLK, feature_width)
    sends = []
    for head in range(heads_here):
        cols = slice(head * HD, (head + 1) * HD)
        sends.append(jnp.stack([kb[:, :, cols], vb[:, :, cols]], axis=1)[asked])

    width = w_out.shape[1] // groups
    w_rel = []
    for shift in range(groups):
        part = lax.dynamic_slice_in_dim(w_out, (group + shift) % groups * width, width, 1)
        w_rel.append(shifted(part, shift) if shift else part)
    mine = [group, group - 2, group + 2, group + 4]
    place = jnp.stack([g % groups for g in mine + [(g % groups) ^ 1 for g in mine]])
    w_rel = jnp.stack(w_rel).reshape(groups, heads_here, HD, width)
    w_cols = w_rel[(group - place) % groups]
    w_heads = [w_cols[:, head].reshape(groups * HD, width) for head in range(heads_here)]

    sends[1], w_heads = lax.optimization_barrier((sends[1], w_heads))
    incoming = [lax.all_to_all(x, "ctx", split_axis=0, concat_axis=0, tiled=True) for x in sends]
    part = None
    for head in range(heads_here):
        attended = attend(head, slots, live, queries, kb, vb, incoming[head])
        part = project(gathered_pieces(attended), w_heads[head], part, jnp.bfloat16 if head else jnp.float32)
        live, part = lax.optimization_barrier((live, part))
    return part


def solution(mesh):
    in_specs = (
        P("ctx", "head"),
        P("ctx", "head"),
        P("ctx", "head"),
        P("ctx", None),
        P("head", None),
    )
    out_specs = P("ctx", "head")
    return jax.shard_map(
        on_device, mesh=mesh, in_specs=in_specs, out_specs=out_specs, check_vma=False
    )
```
